256 devices in a mesh: shard: 32 (over x, z_lo, core), rep: 8 (over z_hi, y).
Axes of the slice: x: 4, y: 4, z: 8 (z_hi: 2, z_lo: 4; z = z_hi * 4 + z_lo), core: 2. Of those that a mesh axis runs over, the one named last changes fastest.
Arguments:
- queries: bfloat16 [8, 4096, 2048], P('rep', 'shard'), may hold values from -20 to 20
- key_vectors: bfloat16 [8, 4096, 2048], P('rep', 'shard'), may hold values from -7.5 to 7.5
- value_vectors: bfloat16 [8, 4096, 2048], P('rep', 'shard'), may hold values from -6 to 6
- neighbor_ids: int32 [8, 32, 2], P('rep', 'shard'), may hold values from 0 to 31, as said below
- upstream: bfloat16 [8, 4096, 2048], P('rep', 'shard'), may hold values from -6 to 6
- w_out: bfloat16 [2048, 2048], P('shard'), may hold values from -0.125 to 0.125
Outputs:
- projected: bfloat16 [8, 4096, 2048], P('rep', 'shard')
- grad_queries: bfloat16 [8, 4096, 2048], P('rep', 'shard')
- grad_keys: bfloat16 [8, 4096, 2048], P('rep', 'shard')
- grad_values: bfloat16 [8, 4096, 2048], P('rep', 'shard')
- grad_w_out: float32 [2048, 2048], P('shard')
The draws below stay inside these ranges and needn't reach their ends.
Inputs may be any that keep to these rules, and one draw needn't show every extreme that they name: neighbor_ids[m, p, 0] is p - 1 if patch p is linked to patch p - 1 and p otherwise; neighbor_ids[m, p, 1] is p + 1 if patch p is linked to patch p + 1 and p otherwise; links are symmetric; patch 0 has no link before it and patch 32 - 1 none after it; patches p and p + 1 are linked whenever p is even.
All inputs are finite; a program needn't handle non-finite values.
Results may differ from the reference program's by a relative error of at most 0.009.
Values may be sent and summed in bfloat16 or wider, within the bound.
A program may use at most 128 MiB of HBM per device.

```python
import jax
import jax.numpy as jnp
from jax import lax

DM = 2048
HEADS = 16
DH = 128
PATCH = 128
P_DEV = 1
HD = 2048
PATCHES = 32
NODES = 4096
MESHES = 8
N_REP = 8


def draw_queries(key, part):
    shape = (N_REP, NODES, HEADS, DH)
    result = 1.5 * jnp.clip(jax.random.normal(jax.random.fold_in(key, 1), shape, jnp.float32), -6.0, 6.0)
    return result.reshape(N_REP, NODES, HEADS * DH).astype(jnp.bfloat16)


def draw_key_vectors(key, part):
    shape = (N_REP, NODES, HEADS, DH)
    result = jnp.clip(jax.random.normal(jax.random.fold_in(key, 2), shape, jnp.float32), -6.0, 6.0)
    return result.reshape(N_REP, NODES, HEADS * DH).astype(jnp.bfloat16)


def draw_neighbor_ids(key, part):
    coins = jax.random.randint(jax.random.fold_in(key, 3), (N_REP, PATCHES), 0, 4)
    index = jnp.arange(PATCHES, dtype=jnp.int32)
    forced = (index + 1) % (2 * P_DEV) == P_DEV
    linked = ((coins > 0) | forced[None, :]) & (index < PATCHES - 1)[None, :]
    before = jnp.concatenate([jnp.zeros((N_REP, 1), jnp.bool_), linked[:, :-1]], axis=1)
    left_ids = jnp.where(before, index[None, :] - 1, index[None, :])
    right_ids = jnp.where(linked, index[None, :] + 1, index[None, :])
    return jnp.stack([left_ids, right_ids], axis=-1).astype(jnp.int32)


def level_of(key, dims, split, smallest, largest):
    level, own = 1.0, jax.random.fold_in(key, 6)
    for axis_at, blocks in split:
        steps = jnp.exp(jax.random.uniform(jax.random.fold_in(own, axis_at), (blocks,), jnp.float32, smallest / len(split), largest / len(split)))
        level = level * jnp.repeat(steps, dims[axis_at] // blocks).reshape([-1 if axis == axis_at else 1 for axis in range(len(dims))])
    return level


def noise(own_key, shape, scale, bound, cuts=(), kind=jnp.bfloat16):
    values = scale * jax.random.normal(own_key, shape, jnp.float32)
    if cuts:
        values = values * level_of(own_key, shape, cuts, -0.22, 0.18)
    return jnp.clip(values, -bound, bound).astype(kind)


def setup_inputs(seed: int = 0) -> dict:
    splits = jax.random.split(jax.random.key(seed), 7)
    queries = draw_queries(jax.random.fold_in(splits[6], 71), 0)
    key_vectors = draw_key_vectors(jax.random.fold_in(splits[6], 71), 0)
    value_vectors = noise(splits[2], (MESHES, NODES, HD), 1.0, 6.0, ((0, 8), (1, 32)))
    neighbor_ids = draw_neighbor_ids(jax.random.fold_in(splits[6], 71), 0)
    upstream = noise(splits[4], (MESHES, NODES, DM), 1.0, 6.0, ((0, 8), (1, 32)))
    w_out = noise(splits[5], (HD, DM), HD ** -0.5, 0.125, ((0, 32),))
    return {"queries": queries, "key_vectors": key_vectors, "value_vectors": value_vectors, "neighbor_ids": neighbor_ids, "upstream": upstream, "w_out": w_out}


def windows_of(rows_in, patch_count):
    blank = jnp.zeros((PATCH, rows_in.shape[1]), rows_in.dtype)
    padded = jnp.concatenate([blank, rows_in, blank], axis=0).reshape(patch_count + 2, PATCH, HEADS, DH)
    return jnp.concatenate([padded[:-2], padded[1:-1], padded[2:]], axis=1)


def spread_terms(terms, patch_count):
    widened = terms.astype(jnp.float32).reshape(patch_count, 3, PATCH, HEADS * DH)
    edges = ((0, 0), (0, 0))
    return (jnp.pad(widened[:, 0], ((0, 2),) + edges) + jnp.pad(widened[:, 1], ((1, 1),) + edges)
            + jnp.pad(widened[:, 2], ((2, 0),) + edges))


def mesh_pass(query_rows, key_rows, value_rows, link_ids, upstream_rows, w_out):
    patch_count = query_rows.shape[0] // PATCH
    node_count = query_rows.shape[0]
    scaling = DH ** -0.5
    exact = lax.Precision.HIGHEST
    patch_ids = jnp.arange(patch_count, dtype=jnp.int32)
    left_ok = link_ids[:, 0] != patch_ids
    right_ok = link_ids[:, 1] != patch_ids
    allowed = jnp.concatenate([jnp.broadcast_to(left_ok[:, None], (patch_count, PATCH)),
                               jnp.ones((patch_count, PATCH), jnp.bool_),
                               jnp.broadcast_to(right_ok[:, None], (patch_count, PATCH))], axis=1)
    key_win = windows_of(key_rows, patch_count).astype(jnp.float32)
    value_win = windows_of(value_rows, patch_count).astype(jnp.float32)
    query_blk = query_rows.reshape(patch_count, PATCH, HEADS, DH).astype(jnp.float32)
    scores = jnp.einsum("pqhd,pkhd->phqk", query_blk, key_win, precision=exact) * scaling
    key_mask = allowed[:, None, None, :]
    highest = jnp.max(jnp.where(key_mask, scores, -jnp.inf), axis=-1)
    numerators = jnp.where(key_mask, jnp.exp(scores - highest[..., None]), 0.0)
    totals = jnp.sum(numerators, axis=-1)
    probabilities = numerators / totals[..., None]
    prob_half = lax.optimization_barrier(probabilities.astype(jnp.bfloat16)).astype(jnp.float32)
    attended = jnp.einsum("phqk,pkhd->pqhd", prob_half, value_win, precision=exact)
    attended = attended.astype(jnp.bfloat16).reshape(node_count, HEADS * DH)
    projected = jnp.dot(attended, w_out, preferred_element_type=jnp.float32).astype(jnp.bfloat16)
    grad_attended = jnp.dot(upstream_rows, w_out.T, preferred_element_type=jnp.float32).astype(jnp.bfloat16)
    weight_term = jnp.dot(attended.T, upstream_rows, preferred_element_type=jnp.float32)
    grad_blk = grad_attended.reshape(patch_count, PATCH, HEADS, DH).astype(jnp.float32)
    prob_grad = jnp.einsum("pqhd,pkhd->phqk", grad_blk, value_win, precision=exact)
    row_delta = jnp.sum(probabilities * prob_grad, axis=-1)
    score_grad = (probabilities * (prob_grad - row_delta[..., None]))
    score_grad = lax.optimization_barrier(score_grad.astype(jnp.bfloat16)).astype(jnp.float32)
    grad_queries = jnp.einsum("phqk,pkhd->pqhd", score_grad, key_win, precision=exact) * scaling
    grad_queries = grad_queries.astype(jnp.bfloat16).reshape(node_count, HEADS * DH)
    key_terms = (jnp.einsum("phqk,pqhd->pkhd", score_grad, query_blk, precision=exact) * scaling).astype(jnp.bfloat16)
    value_terms = jnp.einsum("phqk,pqhd->pkhd", prob_half, grad_blk, precision=exact).astype(jnp.bfloat16)
    grad_keys = spread_terms(key_terms, patch_count)[1:patch_count + 1].astype(jnp.bfloat16).reshape(node_count, HEADS * DH)
    grad_values = spread_terms(value_terms, patch_count)[1:patch_count + 1].astype(jnp.bfloat16).reshape(node_count, HEADS * DH)
    return projected, grad_queries, grad_keys, grad_values, weight_term


def reference(queries, key_vectors, value_vectors, neighbor_ids, upstream, w_out):
    def advance(running, pieces):
        results = mesh_pass(pieces[0], pieces[1], pieces[2], pieces[3], pieces[4], w_out)
        return running + results[4], results[:4]

    start_grad = jnp.zeros((HEADS * DH, DM), jnp.float32)
    summed, stacked = lax.scan(advance, start_grad, (queries, key_vectors, value_vectors, neighbor_ids, upstream))
    factor = float(queries.shape[0] * queries.shape[1]) ** -0.5
    grad_w_out = summed * factor
    return stacked[0], stacked[1], stacked[2], stacked[3], grad_w_out
```

```python
import functools

import jax
import jax.numpy as jnp
from jax import lax
from jax.experimental import pallas as pl
from jax.experimental.pallas import tpu as pltpu
from jax.sharding import PartitionSpec as P

HEADS = 16
DH = 128
PATCH = 128
WIDTH = 2048
HALF = 1024
CHUNKS = 4
CW = WIDTH // CHUNKS
MESH = pl.DeviceIdType.MESH
F32 = jnp.float32
BF16 = jnp.bfloat16


def remote(src, dst, send, recv, target):
    return pltpu.make_async_remote_copy(
        src_ref=src, dst_ref=dst, send_sem=send, recv_sem=recv, device_id=target, device_id_type=MESH
    )


def kernel(
    factor,
    ids_ref,
    q_hbm,
    k_hbm,
    v_hbm,
    u_hbm,
    w_hbm,
    proj_ref,
    gq_ref,
    gk_ref,
    gv_ref,
    gw_ref,
    q_s,
    kw,
    vw,
    ubuf,
    tile,
    gsend,
    grecv,
    att,
    abuf,
    psend,
    precv,
    prob,
    prob_half,
    kts,
    vts,
    ktr,
    vtr,
    gw,
    ds,
    dr,
    xs,
    xr,
    zs,
    zr,
    fs,
    fr,
    local_sem,
    kv_send,
    kv_recv,
    y_send,
    y_recv,
    w_send,
    w_recv,
    t_send,
    t_recv,
    g_send,
    g_recv,
    f_send,
    f_recv,
):
    s = lax.axis_index("shard")
    r = lax.axis_index("rep")
    c = s % 2
    zl = (s // 2) % 4
    x = s // 8
    y = r % 4
    zh = r // 4
    z = zh * 4 + zl
    a = y // 2
    b = y % 2
    par = zl % 2
    zz = zl // 2

    def dev(dx, dy, zpos, core):
        return (dx * 8 + (zpos % 4) * 2 + core, (zpos // 4) * 4 + dy)

    ydev = [dev(x, (y + d) % 4, z, c) for d in range(4)]
    xdev = [dev((x + d) % 4, y, z, c) for d in range(4)]
    zdev = [dev(x, y, (z + d) % 8, c) for d in range(8)]
    sib = dev(x, y, z, 1 - c)
    left = (jnp.maximum(s - 1, 0), r)
    right = (jnp.minimum(s + 1, 31), r)
    has_left = s > 0
    has_right = s < 31

    loads = [
        pltpu.make_async_copy(q_hbm.at[0], q_s, local_sem.at[0]),
        pltpu.make_async_copy(k_hbm.at[0], kw.at[pl.ds(PATCH, PATCH)], local_sem.at[1]),
        pltpu.make_async_copy(v_hbm.at[0], vw.at[pl.ds(PATCH, PATCH)], local_sem.at[2]),
        pltpu.make_async_copy(
            u_hbm.at[0, :, pl.ds(pl.multiple_of(b * HALF, HALF), HALF)], ubuf.at[y], local_sem.at[3]
        ),
    ]
    for copy in loads:
        copy.start()
    wcols = pl.ds(pl.multiple_of(b * HALF, HALF), HALF)
    own_w = pltpu.make_async_copy(w_hbm.at[:, wcols], tile.at[2 * x + zz, c], local_sem.at[4])

    @pl.when(par == a)
    def _():
        own_w.start()

    barrier = pltpu.get_barrier_semaphore()

    def greet(target):
        pl.semaphore_signal(barrier, inc=1, device_id=target, device_id_type=MESH)

    for d in range(1, 4):
        greet(ydev[d])
        greet(xdev[d])
    for d in range(1, 8):
        greet(zdev[d])
    greet(sib)

    @pl.when(has_left)
    def _():
        greet(left)

    @pl.when(has_right)
    def _():
        greet(right)

    for bb in range(2):
        for zlow in range(2):
            for zhigh in range(2):
                sy = 2 * par + bb
                szl = 2 * zz + zlow
                same = (sy == y) & (szl == zl) & (zhigh == zh)

                @pl.when(jnp.logical_not(same))
                def _(sy=sy, szl=szl, zhigh=zhigh):
                    greet(dev(x, sy, zhigh * 4 + szl, c))

    wait_for = (
        14
        + jnp.where(has_left, 1, 0)
        + jnp.where(has_right, 1, 0)
        + jnp.where(par == a, 7, 8)
    )
    pl.semaphore_wait(barrier, wait_for)

    zoff = [1, 7, jnp.where(c == 0, 2, 6)]

    @pl.when(par == a)
    def _():
        for i, d in enumerate(zoff):
            remote(
                w_hbm.at[:, wcols],
                tile.at[2 * x + zz, c],
                w_send.at[i],
                w_recv.at[i],
                dev(x, y, (z + d) % 8, c),
            ).start()

    def halo(i, k, direction):
        src, dst = ((k_hbm, kw), (v_hbm, vw))[k]
        cols = pl.ds(i * CW, CW)
        rows = pl.ds(0 if direction else 2 * PATCH, PATCH)
        index = (i * 2 + k) * 2 + direction
        return remote(
            src.at[0, :, cols],
            dst.at[rows, cols],
            kv_send.at[index],
            kv_recv.at[index],
            right if direction else left,
        )

    for i in range(CHUNKS):
        for k in range(2):

            @pl.when(has_left)
            def _(i=i, k=k):
                halo(i, k, 0).start()

            @pl.when(has_right)
            def _(i=i, k=k):
                halo(i, k, 1).start()

    def ycopy(kind, d, src, dst_buf, slot):
        return remote(src, dst_buf.at[slot], y_send.at[kind, d - 1], y_recv.at[kind, d - 1], ydev[d])

    def u_piece(d):
        bb = ((y + d) % 4) % 2
        return u_hbm.at[0, :, pl.ds(pl.multiple_of(bb * HALF, HALF), HALF)]

    for d in (1, 3, 2):
        ycopy(0, d, u_piece(d), ubuf, y).start()

    def ywait_recv(kind, d, src, dst_buf):
        ycopy(kind, d, src, dst_buf, (y - d + 4) % 4).wait_recv()

    @pl.when(jnp.logical_not(has_left))
    def _():
        kw[0:PATCH, :] = jnp.zeros((PATCH, WIDTH), BF16)
        vw[0:PATCH, :] = jnp.zeros((PATCH, WIDTH), BF16)
        ktr[0] = jnp.zeros((PATCH, WIDTH), BF16)
        vtr[0] = jnp.zeros((PATCH, WIDTH), BF16)

    @pl.when(jnp.logical_not(has_right))
    def _():
        kw[2 * PATCH :, :] = jnp.zeros((PATCH, WIDTH), BF16)
        vw[2 * PATCH :, :] = jnp.zeros((PATCH, WIDTH), BF16)
        ktr[1] = jnp.zeros((PATCH, WIDTH), BF16)
        vtr[1] = jnp.zeros((PATCH, WIDTH), BF16)

    def wz_wait(i):
        d = zoff[i]
        szl = (z - d + 8) % 4
        remote(
            w_hbm.at[:, wcols],
            tile.at[2 * x + szl // 2, c],
            w_send.at[i],
            w_recv.at[i],
            sib,
        ).wait_recv()

    @pl.when(par == a)
    def _():
        own_w.wait()
        wz_wait(2)

    @pl.when(par != a)
    def _():
        wz_wait(0)
        wz_wait(1)

    def wx(d):
        part = tile.at[pl.ds(2 * x, 2), c]
        return remote(part, part, w_send.at[2 + d], w_recv.at[2 + d], xdev[d])

    def wx_wait(d):
        part = tile.at[pl.ds(2 * ((x - d + 4) % 4), 2), c]
        remote(part, part, w_send.at[2 + d], w_recv.at[2 + d], xdev[d]).wait_recv()

    for d in (1, 3, 2):
        wx(d).start()
    for d in (1, 3, 2):
        wx_wait(d)
    to_sib = remote(tile.at[:, c], tile.at[:, c], w_send.at[6], w_recv.at[6], sib)
    to_sib.start()
    from_sib = remote(tile.at[:, 1 - c], tile.at[:, 1 - c], w_send.at[6], w_recv.at[6], sib)
    from_sib.wait_recv()

    loads[3].wait()
    for d in (1, 3, 2):
        ywait_recv(0, d, u_piece(d), ubuf)
    nodes_u = ubuf[...].reshape(4 * PATCH, HALF)
    for j in range(4):
        rows = tile[2 * j : 2 * j + 2].reshape(256, HALF)
        part = lax.dot_general(nodes_u, rows, (((1,), (1,)), ((), ())), preferred_element_type=F32)
        gsend[:, :, 256 * j : 256 * j + 256] = part.astype(BF16).reshape(4, PATCH, 256)
    for d in (1, 3, 2):
        ycopy(1, d, gsend.at[(y + d) % 4], grecv, y).start()
    grecv[y] = gsend[y]

    for copy in loads[:3]:
        copy.wait()
    left_ok = ids_ref[0, 0, 0] != s
    right_ok = ids_ref[0, 0, 1] != s
    at = lax.broadcasted_iota(jnp.int32, (PATCH, 3 * PATCH), 1)
    allowed = ((at >= PATCH) | left_ok) & ((at < 2 * PATCH) | right_ok)
    scaling = DH ** (-0.5)

    def forward_head(h, half, t):
        cols = pl.ds(pl.multiple_of(h * DH, DH), DH)
        scores = (
            lax.dot_general(q_s[:, cols], kw[:, cols], (((1,), (1,)), ((), ())), preferred_element_type=F32)
            * scaling
        )
        highest = jnp.max(jnp.where(allowed, scores, -jnp.inf), axis=-1, keepdims=True)
        numer = jnp.where(allowed, jnp.exp(scores - highest), 0.0)
        total = jnp.sum(numer, axis=-1, keepdims=True)
        p = numer / total
        ph = p.astype(BF16)
        prob[h] = p
        prob_half[h] = ph
        out = jnp.dot(ph, vw[:, cols], preferred_element_type=F32)
        att[half, :, pl.ds(pl.multiple_of(t * DH, DH), DH)] = out.astype(BF16)

    per = HEADS // 2 // CHUNKS

    for i in range(CHUNKS):
        for k in range(2):

            @pl.when(has_left)
            def _(i=i, k=k):
                halo(i, k, 1).wait_recv()

            @pl.when(has_right)
            def _(i=i, k=k):
                halo(i, k, 0).wait_recv()

        @pl.loop(i * per, (i + 1) * per)
        def _(t):
            for half in range(2):
                forward_head(2 * t + half, half, t)

    def a_piece(d):
        return att.at[((y + d) % 4) // 2]

    for d in (1, 3, 2):
        ycopy(2, d, a_piece(d), abuf, y).start()
    abuf[y] = att[a]

    for d in (1, 3, 2):
        ywait_recv(1, d, gsend.at[(y + d) % 4], grecv)

    def term(i, k, direction):
        src, dst = ((kts, ktr), (vts, vtr))[k]
        cols = pl.ds(i * CW, CW)
        index = (i * 2 + k) * 2 + direction
        return remote(
            src.at[2 * direction, :, cols],
            dst.at[1 - direction, :, cols],
            t_send.at[index],
            t_recv.at[index],
            right if direction else left,
        )

    def backward_head(h, half, t):
        cols = pl.ds(pl.multiple_of(h * DH, DH), DH)
        tc = pl.ds(pl.multiple_of(t * DH, DH), DH)
        ga = (grecv[2 * half, :, tc].astype(F32) + grecv[2 * half + 1, :, tc].astype(F32)).astype(BF16)
        p = prob[h]
        pg = lax.dot_general(ga, vw[:, cols], (((1,), (1,)), ((), ())), preferred_element_type=F32)
        delta = jnp.sum(p * pg, axis=-1, keepdims=True)
        sg = (p * (pg - delta)).astype(BF16)
        gq_ref[0, :, cols] = (jnp.dot(sg, kw[:, cols], preferred_element_type=F32) * scaling).astype(BF16)
        kt = (
            lax.dot_general(sg, q_s[:, cols], (((0,), (0,)), ((), ())), preferred_element_type=F32) * scaling
        ).astype(BF16)
        vt = lax.dot_general(
            prob_half[h], ga, (((0,), (0,)), ((), ())), preferred_element_type=F32
        ).astype(BF16)
        kts[:, :, cols] = kt.reshape(3, PATCH, DH)
        vts[:, :, cols] = vt.reshape(3, PATCH, DH)

    for i in range(CHUNKS):

        @pl.loop(i * per, (i + 1) * per)
        def _(t):
            for half in range(2):
                backward_head(2 * t + half, half, t)

        for k in range(2):

            @pl.when(has_left)
            def _(i=i, k=k):
                term(i, k, 0).start()

            @pl.when(has_right)
            def _(i=i, k=k):
                term(i, k, 1).start()

    for d in (1, 3, 2):
        ywait_recv(2, d, a_piece(d), abuf)
    nodes_u = ubuf[...].reshape(4 * PATCH, HALF)
    for j in range(4):
        cols_a = abuf[:, :, 256 * j : 256 * j + 256].reshape(4 * PATCH, 256)
        part = lax.dot_general(cols_a, nodes_u, (((0,), (0,)), ((), ())), preferred_element_type=F32)
        gw[2 * j : 2 * j + 2] = part.reshape(2, 2, 64, HALF)
    ds[...] = gw[:, 1 - c].astype(BF16)
    d_copy = remote(ds, dr, g_send.at[0], g_recv.at[0], sib)
    d_copy.start()

    nodes_a = abuf[...].reshape(4 * PATCH, HALF)
    weights = tile[...].reshape(HALF, HALF)
    for j in range(4):
        part = jnp.dot(nodes_a, weights[:, 256 * j : 256 * j + 256], preferred_element_type=F32)
        psend[:, :, 256 * j : 256 * j + 256] = part.astype(BF16).reshape(4, PATCH, 256)
    for d in (1, 3, 2):
        ycopy(3, d, psend.at[(y + d) % 4], precv, y).start()
    precv[y] = psend[y]

    d_copy.wait_recv()
    xs[...] = (gw[:, c] + dr[...].astype(F32)).astype(BF16)

    def x_copy(d):
        return remote(
            xs.at[pl.ds(2 * ((x + d) % 4), 2)], xr.at[d - 1], g_send.at[d], g_recv.at[d], xdev[d]
        )

    for d in (1, 3, 2):
        x_copy(d).start()
    for d in (1, 3, 2):
        x_copy(d).wait_recv()
    own = gw[pl.ds(2 * x, 2), c] + dr[pl.ds(2 * x, 2)].astype(F32)
    for d in range(3):
        own += xr[d].astype(F32)
    zs[...] = own.astype(BF16)

    def z_piece(d):
        to = (z + d) % 8
        quarter = (to // 4) * 2 + to % 2
        return zs.at[(to % 4) // 2, pl.ds(pl.multiple_of(quarter * 16, 16), 16)]

    def z_copy(d):
        return remote(z_piece(d), zr.at[d - 1], g_send.at[3 + d], g_recv.at[3 + d], zdev[d])

    for d in (4, 3, 5, 2, 6, 1, 7):
        z_copy(d).start()
    quarter = zh * 2 + par
    mine = zs[zz, pl.ds(pl.multiple_of(quarter * 16, 16), 16)].astype(F32)
    for d in range(1, 8):
        z_copy(d).wait_recv()
    for d in range(7):
        mine += zr[d].astype(F32)
    fs[...] = (mine * factor).astype(BF16)

    szl = 2 * zz + a

    def spread(zhigh, dy, slot):
        return remote(
            fs,
            fr.at[quarter, b],
            f_send.at[slot],
            f_recv.at[2 * quarter + b],
            dev(x, dy, zhigh * 4 + szl, c),
        )

    def spread_same(zhigh, dy):
        return (par == a) & (zhigh == zh) & (dy == y)

    for zhigh in range(2):
        for dy in range(4):

            @pl.when(jnp.logical_not(spread_same(zhigh, dy)))
            def _(zhigh=zhigh, dy=dy):
                spread(zhigh, dy, zhigh * 4 + dy).start()

    @pl.when(par == a)
    def _():
        fr[quarter, b] = fs[...]

    for d in (1, 3, 2):
        ywait_recv(3, d, psend.at[(y + d) % 4], precv)
    for bb in range(2):
        proj_ref[0, :, bb * HALF : (bb + 1) * HALF] = (
            precv[bb].astype(F32) + precv[2 + bb].astype(F32)
        ).astype(BF16)

    for i in range(CHUNKS):
        for k in range(2):

            @pl.when(has_left)
            def _(i=i, k=k):
                term(i, k, 1).wait_recv()

            @pl.when(has_right)
            def _(i=i, k=k):
                term(i, k, 0).wait_recv()

    gk_ref[0] = (kts[1].astype(F32) + ktr[0].astype(F32) + ktr[1].astype(F32)).astype(BF16)
    gv_ref[0] = (vts[1].astype(F32) + vtr[0].astype(F32) + vtr[1].astype(F32)).astype(BF16)

    for qq in range(4):
        for bb in range(2):
            same = (par == a) & (qq == quarter) & (bb == b)

            @pl.when(jnp.logical_not(same))
            def _(qq=qq, bb=bb):
                remote(
                    fs, fr.at[qq, bb], f_send.at[0], f_recv.at[2 * qq + bb], sib
                ).wait_recv()

    for qq in range(4):
        for bb in range(2):
            gw_ref[16 * qq : 16 * qq + 16, bb * HALF : (bb + 1) * HALF] = fr[qq, bb].astype(F32)

    @pl.when(par == a)
    def _():
        for i in range(3):
            remote(w_hbm.at[:, wcols], tile.at[2 * x + zz, c], w_send.at[i], w_recv.at[i], sib).wait_send()

    for d in range(1, 4):
        wx(d).wait_send()
        ycopy(0, d, u_piece(d), ubuf, y).wait_send()
        ycopy(1, d, gsend.at[(y + d) % 4], grecv, y).wait_send()
        ycopy(2, d, a_piece(d), abuf, y).wait_send()
        ycopy(3, d, psend.at[(y + d) % 4], precv, y).wait_send()
        x_copy(d).wait_send()
    to_sib.wait_send()
    d_copy.wait_send()
    for d in range(1, 8):
        z_copy(d).wait_send()
    for i in range(CHUNKS):
        for k in range(2):

            @pl.when(has_left)
            def _(i=i, k=k):
                halo(i, k, 0).wait_send()
                term(i, k, 0).wait_send()

            @pl.when(has_right)
            def _(i=i, k=k):
                halo(i, k, 1).wait_send()
                term(i, k, 1).wait_send()

    for zhigh in range(2):
        for dy in range(4):

            @pl.when(jnp.logical_not(spread_same(zhigh, dy)))
            def _(zhigh=zhigh, dy=dy):
                spread(zhigh, dy, zhigh * 4 + dy).wait_send()


def per_device(queries, key_vectors, value_vectors, neighbor_ids, upstream, w_out):
    factor = float(8 * 4096) ** (-0.5)
    rows = jax.ShapeDtypeStruct((1, PATCH, WIDTH), BF16)
    dma = pltpu.SemaphoreType.DMA
    vmem = pltpu.VMEM
    out = pl.pallas_call(
        functools.partial(kernel, factor),
        out_shape=(rows, rows, rows, rows, jax.ShapeDtypeStruct((64, WIDTH), F32)),
        in_specs=[pl.BlockSpec(memory_space=pltpu.SMEM)] + [pl.BlockSpec(memory_space=pl.ANY)] * 5,
        out_specs=[pl.BlockSpec(memory_space=pltpu.VMEM)] * 5,
        scratch_shapes=[
            vmem((PATCH, WIDTH), BF16),
            vmem((3 * PATCH, WIDTH), BF16),
            vmem((3 * PATCH, WIDTH), BF16),
            vmem((4, PATCH, HALF), BF16),
            vmem((8, 2, 64, HALF), BF16),
            vmem((4, PATCH, HALF), BF16),
            vmem((4, PATCH, HALF), BF16),
            vmem((2, PATCH, HALF), BF16),
            vmem((4, PATCH, HALF), BF16),
            vmem((4, PATCH, HALF), BF16),
            vmem((4, PATCH, HALF), BF16),
            vmem((HEADS, PATCH, 3 * PATCH), F32),
            vmem((HEADS, PATCH, 3 * PATCH), BF16),
            vmem((3, PATCH, WIDTH), BF16),
            vmem((3, PATCH, WIDTH), BF16),
            vmem((2, PATCH, WIDTH), BF16),
            vmem((2, PATCH, WIDTH), BF16),
            vmem((8, 2, 64, HALF), F32),
            vmem((8, 64, HALF), BF16),
            vmem((8, 64, HALF), BF16),
            vmem((8, 64, HALF), BF16),
            vmem((3, 2, 64, HALF), BF16),
            vmem((2, 64, HALF), BF16),
            vmem((7, 16, HALF), BF16),
            vmem((16, HALF), BF16),
            vmem((4, 2, 16, HALF), BF16),
            dma((5,)),
            dma((4 * CHUNKS,)),
            dma((4 * CHUNKS,)),
            dma((4, 3)),
            dma((4, 3)),
            dma((7,)),
            dma((7,)),
            dma((4 * CHUNKS,)),
            dma((4 * CHUNKS,)),
            dma((11,)),
            dma((11,)),
            dma((8,)),
            dma((8,)),
        ],
        compiler_params=pltpu.CompilerParams(
            collective_id=0, has_side_effects=True, vmem_limit_bytes=56 * 1024 * 1024
        ),
        cost_estimate=pl.CostEstimate(flops=5_000_000_000, bytes_accessed=6_000_000, transcendentals=800_000),
        name="mesh_attention",
    )(neighbor_ids, queries, key_vectors, value_vectors, upstream, w_out)
    return tuple(out)


def solution(mesh):
    rows = P("rep", "shard", None)
    return jax.shard_map(
        per_device,
        mesh=mesh,
        in_specs=(rows, rows, rows, rows, rows, P("shard", None)),
        out_specs=(rows, rows, rows, rows, P("shard", None)),
        check_vma=False,
    )
```

```python
import functools

import jax
import jax.numpy as jnp
from jax import lax
from jax.experimental import pallas as pl
from jax.experimental.pallas import tpu as pltpu
from jax.sharding import PartitionSpec as P

HEADS = 16
DH = 128
PATCH = 128
WIDTH = 2048
HALF = 1024
CHUNKS = 4
CW = WIDTH // CHUNKS
TW = HALF // CHUNKS
ORDER = (0, 1, 3, 2)
MESH = pl.DeviceIdType.MESH
F32 = jnp.float32
BF16 = jnp.bfloat16


def remote(src, dst, send, recv, target):
    return pltpu.make_async_remote_copy(
        src_ref=src, dst_ref=dst, send_sem=send, recv_sem=recv, device_id=target, device_id_type=MESH
    )


def kernel(
    factor,
    ids_ref,
    q_hbm,
    k_hbm,
    v_hbm,
    u_hbm,
    w_hbm,
    proj_ref,
    gq_ref,
    gk_ref,
    gv_ref,
    gw_ref,
    q_s,
    kw,
    vw,
    ubuf,
    tile,
    gsend,
    grecv,
    att,
    abuf,
    psend,
    precv,
    prob,
    prob_half,
    kts,
    vts,
    ktr,
    vtr,
    gw,
    ds,
    dr,
    xs,
    xr,
    zs,
    zr,
    fs,
    fr,
    local_sem,
    kv_send,
    kv_recv,
    y_send,
    y_recv,
    a_send,
    a_recv,
    gy_send,
    gy_recv,
    wd_send,
    wd_recv,
    w_send,
    w_recv,
    t_send,
    t_recv,
    g_send,
    g_recv,
    f_send,
    f_recv,
):
    s = lax.axis_index("shard")
    r = lax.axis_index("rep")
    c = s % 2
    zl = (s // 2) % 4
    x = s // 8
    y = r % 4
    zh = r // 4
    z = zh * 4 + zl
    a = y // 2
    b = y % 2
    par = zl % 2
    zz = zl // 2

    def dev(dx, dy, zpos, core):
        return (dx * 8 + (zpos % 4) * 2 + core, (zpos // 4) * 4 + dy)

    ydev = [dev(x, (y + d) % 4, z, c) for d in range(4)]
    xdev = [dev((x + d) % 4, y, z, c) for d in range(4)]
    zdev = [dev(x, y, (z + d) % 8, c) for d in range(8)]
    sib = dev(x, y, z, 1 - c)
    left = (jnp.maximum(s - 1, 0), r)
    right = (jnp.minimum(s + 1, 31), r)
    x_left = jnp.maximum(s - 1, 0) // 8
    x_right = jnp.minimum(s + 1, 31) // 8
    has_left = s > 0
    has_right = s < 31

    loads = [
        pltpu.make_async_copy(q_hbm.at[0], q_s, local_sem.at[0]),
        pltpu.make_async_copy(k_hbm.at[0], kw.at[pl.ds(PATCH, PATCH)], local_sem.at[1]),
        pltpu.make_async_copy(v_hbm.at[0], vw.at[pl.ds(PATCH, PATCH)], local_sem.at[2]),
        pltpu.make_async_copy(
            u_hbm.at[0, :, pl.ds(pl.multiple_of(b * HALF, HALF), HALF)], ubuf.at[y], local_sem.at[3]
        ),
    ]
    for copy in loads:
        copy.start()
    wcols = pl.ds(pl.multiple_of(b * HALF, HALF), HALF)
    own_w = pltpu.make_async_copy(w_hbm.at[:, wcols], tile.at[2 * x + zz, c], local_sem.at[4])

    @pl.when(par == a)
    def _():
        own_w.start()

    barrier = pltpu.get_barrier_semaphore()

    def greet(target):
        pl.semaphore_signal(barrier, inc=1, device_id=target, device_id_type=MESH)

    for d in range(1, 4):
        greet(ydev[d])
        greet(xdev[d])
    for d in range(1, 8):
        greet(zdev[d])
    greet(sib)

    @pl.when(has_left)
    def _():
        greet(left)

    @pl.when(has_right)
    def _():
        greet(right)

    for bb in range(2):
        for zlow in range(2):
            for zhigh in range(2):
                sy = 2 * par + bb
                szl = 2 * zz + zlow
                same = (sy == y) & (szl == zl) & (zhigh == zh)

                @pl.when(jnp.logical_not(same))
                def _(sy=sy, szl=szl, zhigh=zhigh):
                    greet(dev(x, sy, zhigh * 4 + szl, c))

    wait_for = (
        14
        + jnp.where(has_left, 1, 0)
        + jnp.where(has_right, 1, 0)
        + jnp.where(par == a, 7, 8)
    )
    pl.semaphore_wait(barrier, wait_for)

    zoff = [1, 7, jnp.where(c == 0, 2, 6)]

    @pl.when(par == a)
    def _():
        for i, d in enumerate(zoff):
            remote(
                w_hbm.at[:, wcols],
                tile.at[2 * x + zz, c],
                w_send.at[i],
                w_recv.at[i],
                dev(x, y, (z + d) % 8, c),
            ).start()

    def chunk(at_x, i):
        return (at_x + ORDER[i]) % 4

    def halo(i, k, direction, at_x):
        src, dst = ((k_hbm, kw), (v_hbm, vw))[k]
        cols = pl.ds(pl.multiple_of(chunk(at_x, i) * CW, CW), CW)
        rows = pl.ds(0 if direction else 2 * PATCH, PATCH)
        index = (i * 2 + k) * 2 + direction
        return remote(
            src.at[0, :, cols],
            dst.at[rows, cols],
            kv_send.at[index],
            kv_recv.at[index],
            right if direction else left,
        )

    def halo_start(i):
        for k in range(2):

            @pl.when(has_left)
            def _(k=k):
                halo(i, k, 0, x_left).start()

            @pl.when(has_right)
            def _(k=k):
                halo(i, k, 1, x_right).start()

    def halo_wait(i):
        for k in range(2):

            @pl.when(has_left)
            def _(k=k):
                halo(i, k, 1, x).wait_recv()

            @pl.when(has_right)
            def _(k=k):
                halo(i, k, 0, x).wait_recv()

    for i in range(CHUNKS):
        halo_start(i)

    def ycopy(kind, d, src, dst_buf, slot):
        return remote(src, dst_buf.at[slot], y_send.at[kind, d - 1], y_recv.at[kind, d - 1], ydev[d])

    def u_piece(d):
        bb = ((y + d) % 4) % 2
        return u_hbm.at[0, :, pl.ds(pl.multiple_of(bb * HALF, HALF), HALF)]

    for d in (1, 3, 2):
        ycopy(0, d, u_piece(d), ubuf, y).start()

    def ywait_recv(kind, d, src, dst_buf):
        ycopy(kind, d, src, dst_buf, (y - d + 4) % 4).wait_recv()

    @pl.when(jnp.logical_not(has_left))
    def _():
        kw[0:PATCH, :] = jnp.zeros((PATCH, WIDTH), BF16)
        vw[0:PATCH, :] = jnp.zeros((PATCH, WIDTH), BF16)
        ktr[0] = jnp.zeros((PATCH, WIDTH), BF16)
        vtr[0] = jnp.zeros((PATCH, WIDTH), BF16)

    @pl.when(jnp.logical_not(has_right))
    def _():
        kw[2 * PATCH :, :] = jnp.zeros((PATCH, WIDTH), BF16)
        vw[2 * PATCH :, :] = jnp.zeros((PATCH, WIDTH), BF16)
        ktr[1] = jnp.zeros((PATCH, WIDTH), BF16)
        vtr[1] = jnp.zeros((PATCH, WIDTH), BF16)

    def wz_wait(i):
        d = zoff[i]
        szl = (z - d + 8) % 4
        remote(
            w_hbm.at[:, wcols],
            tile.at[2 * x + szl // 2, c],
            w_send.at[i],
            w_recv.at[i],
            sib,
        ).wait_recv()

    @pl.when(par == a)
    def _():
        own_w.wait()
        wz_wait(2)

    @pl.when(par != a)
    def _():
        wz_wait(0)
        wz_wait(1)

    def wx(d):
        part = tile.at[pl.ds(2 * x, 2), c]
        return remote(part, part, w_send.at[2 + d], w_recv.at[2 + d], xdev[d])

    def wx_wait(d):
        part = tile.at[pl.ds(2 * ((x - d + 4) % 4), 2), c]
        remote(part, part, w_send.at[2 + d], w_recv.at[2 + d], xdev[d]).wait_recv()

    for d in (1, 3, 2):
        wx(d).start()

    for copy in loads[:3]:
        copy.wait()
    left_ok = ids_ref[0, 0, 0] != s
    right_ok = ids_ref[0, 0, 1] != s
    at = lax.broadcasted_iota(jnp.int32, (PATCH, 3 * PATCH), 1)
    allowed = ((at >= PATCH) | left_ok) & ((at < 2 * PATCH) | right_ok)
    scaling = DH ** (-0.5)
    per = HEADS // 2 // CHUNKS

    def forward_head(h, half, t):
        cols = pl.ds(pl.multiple_of(h * DH, DH), DH)
        scores = (
            lax.dot_general(q_s[:, cols], kw[:, cols], (((1,), (1,)), ((), ())), preferred_element_type=F32)
            * scaling
        )
        highest = jnp.max(jnp.where(allowed, scores, -jnp.inf), axis=-1, keepdims=True)
        numer = jnp.where(allowed, jnp.exp(scores - highest), 0.0)
        total = jnp.sum(numer, axis=-1, keepdims=True)
        p = numer / total
        ph = p.astype(BF16)
        prob[h] = p
        prob_half[h] = ph
        out = jnp.dot(ph, vw[:, cols], preferred_element_type=F32)
        att[half, :, pl.ds(pl.multiple_of(t * DH, DH), DH)] = out.astype(BF16)

    def tcols(i):
        return pl.ds(pl.multiple_of(chunk(x, i) * TW, TW), TW)

    def a_copy(i, d, slot):
        return remote(
            att.at[((y + d) % 4) // 2, :, tcols(i)],
            abuf.at[slot, :, tcols(i)],
            a_send.at[i, d - 1],
            a_recv.at[i, d - 1],
            ydev[d],
        )

    def forward(i):
        halo_wait(i)
        first = chunk(x, i) * per

        @pl.loop(0, per)
        def _(n):
            for half in range(2):
                forward_head(2 * (first + n) + half, half, first + n)

        for d in (1, 3, 2):
            a_copy(i, d, y).start()
        abuf[y, :, tcols(i)] = att[a, :, tcols(i)]

    def wd_copy(i, core):
        part = tile.at[pl.ds(2 * chunk(x, i), 2), core]
        return remote(part, part, wd_send.at[i], wd_recv.at[i], sib)

    def tile_ready(i):
        if i > 0:
            wx_wait((4 - ORDER[i]) % 4)
        wd_copy(i, c).start()

    def g_copy(i, d, slot):
        return remote(
            gsend.at[(y + d) % 4, :, tcols(i)],
            grecv.at[slot, :, tcols(i)],
            gy_send.at[i, d - 1],
            gy_recv.at[i, d - 1],
            ydev[d],
        )

    def upstream_part(i):
        wd_copy(i, 1 - c).wait_recv()
        rows = tile[pl.ds(2 * chunk(x, i), 2)].reshape(TW, HALF)
        nodes = ubuf[...].reshape(4 * PATCH, HALF)
        part = lax.dot_general(nodes, rows, (((1,), (1,)), ((), ())), preferred_element_type=F32)
        gsend[:, :, tcols(i)] = part.astype(BF16).reshape(4, PATCH, TW)
        for d in (1, 3, 2):
            g_copy(i, d, y).start()
        grecv[y, :, tcols(i)] = gsend[y, :, tcols(i)]

    def d_copy(i):
        return remote(ds.at[i], dr.at[i], g_send.at[i], g_recv.at[i], sib)

    def x_copy(i):
        d = ORDER[i]
        return remote(xs.at[i - 1], xr.at[d - 1], g_send.at[3 + d], g_recv.at[3 + d], xdev[d])

    def gradient(i):
        for d in (1, 3, 2):
            a_copy(i, d, (y - d + 4) % 4).wait_recv()
        cols_a = abuf[:, :, tcols(i)].reshape(4 * PATCH, TW)
        nodes_u = ubuf[...].reshape(4 * PATCH, HALF)
        part = lax.dot_general(cols_a, nodes_u, (((0,), (0,)), ((), ())), preferred_element_type=F32)
        gw[i] = part.reshape(2, 2, 64, HALF)
        ds[i] = gw[i, :, 1 - c].astype(BF16)
        d_copy(i).start()

    def over_x(i):
        d_copy(i).wait_recv()
        xs[i - 1] = (gw[i, :, c] + dr[i].astype(F32)).astype(BF16)
        x_copy(i).start()

    def term(i, k, direction, at_x):
        src, dst = ((kts, ktr), (vts, vtr))[k]
        cols = pl.ds(pl.multiple_of(chunk(at_x, i) * CW, CW), CW)
        index = (i * 2 + k) * 2 + direction
        return remote(
            src.at[2 * direction, :, cols],
            dst.at[1 - direction, :, cols],
            t_send.at[index],
            t_recv.at[index],
            right if direction else left,
        )

    def backward_head(h, half, t):
        cols = pl.ds(pl.multiple_of(h * DH, DH), DH)
        tc = pl.ds(pl.multiple_of(t * DH, DH), DH)
        ga = (grecv[2 * half, :, tc].astype(F32) + grecv[2 * half + 1, :, tc].astype(F32)).astype(BF16)
        p = prob[h]
        pg = lax.dot_general(ga, vw[:, cols], (((1,), (1,)), ((), ())), preferred_element_type=F32)
        delta = jnp.sum(p * pg, axis=-1, keepdims=True)
        sg = (p * (pg - delta)).astype(BF16)
        gq_ref[0, :, cols] = (jnp.dot(sg, kw[:, cols], preferred_element_type=F32) * scaling).astype(BF16)
        kt = (
            lax.dot_general(sg, q_s[:, cols], (((0,), (0,)), ((), ())), preferred_element_type=F32) * scaling
        ).astype(BF16)
        vt = lax.dot_general(
            prob_half[h], ga, (((0,), (0,)), ((), ())), preferred_element_type=F32
        ).astype(BF16)
        kts[:, :, cols] = kt.reshape(3, PATCH, DH)
        vts[:, :, cols] = vt.reshape(3, PATCH, DH)

    def backward(i):
        first = chunk(x, i) * per
        for d in (1, 3, 2):
            g_copy(i, d, (y - d + 4) % 4).wait_recv()

        @pl.loop(0, per)
        def _(n):
            for half in range(2):
                backward_head(2 * (first + n) + half, half, first + n)

        for k in range(2):

            @pl.when(has_left)
            def _(k=k):
                term(i, k, 0, x).start()

            @pl.when(has_right)
            def _(k=k):
                term(i, k, 1, x).start()

    tile_ready(0)
    forward(0)
    loads[3].wait()
    for d in (1, 3, 2):
        ywait_recv(0, d, u_piece(d), ubuf)
    upstream_part(0)
    tile_ready(1)
    forward(1)
    upstream_part(1)
    backward(0)
    tile_ready(2)
    forward(2)
    upstream_part(2)
    gradient(0)
    backward(1)
    tile_ready(3)
    forward(3)
    upstream_part(3)
    gradient(1)
    gradient(2)
    over_x(1)
    backward(2)
    gradient(3)
    over_x(2)
    over_x(3)

    nodes_a = abuf[...].reshape(4 * PATCH, HALF)
    weights = tile[...].reshape(HALF, HALF)
    for j in range(4):
        part = jnp.dot(nodes_a, weights[:, 256 * j : 256 * j + 256], preferred_element_type=F32)
        psend[:, :, 256 * j : 256 * j + 256] = part.astype(BF16).reshape(4, PATCH, 256)
    for d in (1, 3, 2):
        ycopy(1, d, psend.at[(y + d) % 4], precv, y).start()
    precv[y] = psend[y]

    backward(3)

    d_copy(0).wait_recv()
    own = gw[0, :, c] + dr[0].astype(F32)
    for i in range(1, CHUNKS):
        x_copy(i).wait_recv()
    for d in range(3):
        own += xr[d].astype(F32)
    zs[...] = own.astype(BF16)

    def z_piece(d):
        to = (z + d) % 8
        quarter = (to // 4) * 2 + to % 2
        return zs.at[(to % 4) // 2, pl.ds(pl.multiple_of(quarter * 16, 16), 16)]

    def z_copy(d):
        return remote(z_piece(d), zr.at[d - 1], g_send.at[6 + d], g_recv.at[6 + d], zdev[d])

    for d in (4, 3, 5, 2, 6, 1, 7):
        z_copy(d).start()

    quarter = zh * 2 + par
    mine = zs[zz, pl.ds(pl.multiple_of(quarter * 16, 16), 16)].astype(F32)
    for d in range(1, 8):
        z_copy(d).wait_recv()
    for d in range(7):
        mine += zr[d].astype(F32)
    fs[...] = (mine * factor).astype(BF16)

    szl = 2 * zz + a

    def spread(zhigh, dy, slot):
        return remote(
            fs,
            fr.at[quarter, b],
            f_send.at[slot],
            f_recv.at[2 * quarter + b],
            dev(x, dy, zhigh * 4 + szl, c),
        )

    def spread_same(zhigh, dy):
        return (par == a) & (zhigh == zh) & (dy == y)

    for zhigh in range(2):
        for dy in range(4):

            @pl.when(jnp.logical_not(spread_same(zhigh, dy)))
            def _(zhigh=zhigh, dy=dy):
                spread(zhigh, dy, zhigh * 4 + dy).start()

    @pl.when(par == a)
    def _():
        fr[quarter, b] = fs[...]

    for d in (1, 3, 2):
        ywait_recv(1, d, psend.at[(y + d) % 4], precv)
    for bb in range(2):
        proj_ref[0, :, bb * HALF : (bb + 1) * HALF] = (
            precv[bb].astype(F32) + precv[2 + bb].astype(F32)
        ).astype(BF16)

    for i in range(CHUNKS):
        for k in range(2):

            @pl.when(has_left)
            def _(i=i, k=k):
                term(i, k, 1, x_left).wait_recv()

            @pl.when(has_right)
            def _(i=i, k=k):
                term(i, k, 0, x_right).wait_recv()

    gk_ref[0] = (kts[1].astype(F32) + ktr[0].astype(F32) + ktr[1].astype(F32)).astype(BF16)
    gv_ref[0] = (vts[1].astype(F32) + vtr[0].astype(F32) + vtr[1].astype(F32)).astype(BF16)

    for qq in range(4):
        for bb in range(2):
            same = (par == a) & (qq == quarter) & (bb == b)

            @pl.when(jnp.logical_not(same))
            def _(qq=qq, bb=bb):
                remote(
                    fs, fr.at[qq, bb], f_send.at[0], f_recv.at[2 * qq + bb], sib
                ).wait_recv()

    for qq in range(4):
        for bb in range(2):
            gw_ref[16 * qq : 16 * qq + 16, bb * HALF : (bb + 1) * HALF] = fr[qq, bb].astype(F32)

    @pl.when(par == a)
    def _():
        for i in range(3):
            remote(w_hbm.at[:, wcols], tile.at[2 * x + zz, c], w_send.at[i], w_recv.at[i], sib).wait_send()

    for d in range(1, 4):
        wx(d).wait_send()
        ycopy(0, d, u_piece(d), ubuf, y).wait_send()
        for i in range(CHUNKS):
            a_copy(i, d, y).wait_send()
            g_copy(i, d, y).wait_send()
        ycopy(1, d, psend.at[(y + d) % 4], precv, y).wait_send()
        x_copy(d).wait_send()
    for i in range(CHUNKS):
        d_copy(i).wait_send()
        wd_copy(i, c).wait_send()
    for d in range(1, 8):
        z_copy(d).wait_send()
    for i in range(CHUNKS):
        for k in range(2):

            @pl.when(has_left)
            def _(i=i, k=k):
                halo(i, k, 0, x_left).wait_send()
                term(i, k, 0, x).wait_send()

            @pl.when(has_right)
            def _(i=i, k=k):
                halo(i, k, 1, x_right).wait_send()
                term(i, k, 1, x).wait_send()

    for zhigh in range(2):
        for dy in range(4):

            @pl.when(jnp.logical_not(spread_same(zhigh, dy)))
            def _(zhigh=zhigh, dy=dy):
                spread(zhigh, dy, zhigh * 4 + dy).wait_send()


def per_device(queries, key_vectors, value_vectors, neighbor_ids, upstream, w_out):
    factor = float(8 * 4096) ** (-0.5)
    rows = jax.ShapeDtypeStruct((1, PATCH, WIDTH), BF16)
    dma = pltpu.SemaphoreType.DMA
    vmem = pltpu.VMEM
    out = pl.pallas_call(
        functools.partial(kernel, factor),
        out_shape=(rows, rows, rows, rows, jax.ShapeDtypeStruct((64, WIDTH), F32)),
        in_specs=[pl.BlockSpec(memory_space=pltpu.SMEM)] + [pl.BlockSpec(memory_space=pl.ANY)] * 5,
        out_specs=[pl.BlockSpec(memory_space=pltpu.VMEM)] * 5,
        scratch_shapes=[
            vmem((PATCH, WIDTH), BF16),
            vmem((3 * PATCH, WIDTH), BF16),
            vmem((3 * PATCH, WIDTH), BF16),
            vmem((4, PATCH, HALF), BF16),
            vmem((8, 2, 64, HALF), BF16),
            vmem((4, PATCH, HALF), BF16),
            vmem((4, PATCH, HALF), BF16),
            vmem((2, PATCH, HALF), BF16),
            vmem((4, PATCH, HALF), BF16),
            vmem((4, PATCH, HALF), BF16),
            vmem((4, PATCH, HALF), BF16),
            vmem((HEADS, PATCH, 3 * PATCH), F32),
            vmem((HEADS, PATCH, 3 * PATCH), BF16),
            vmem((3, PATCH, WIDTH), BF16),
            vmem((3, PATCH, WIDTH), BF16),
            vmem((2, PATCH, WIDTH), BF16),
            vmem((2, PATCH, WIDTH), BF16),
            vmem((CHUNKS, 2, 2, 64, HALF), F32),
            vmem((CHUNKS, 2, 64, HALF), BF16),
            vmem((CHUNKS, 2, 64, HALF), BF16),
            vmem((3, 2, 64, HALF), BF16),
            vmem((3, 2, 64, HALF), BF16),
            vmem((2, 64, HALF), BF16),
            vmem((7, 16, HALF), BF16),
            vmem((16, HALF), BF16),
            vmem((4, 2, 16, HALF), BF16),
            dma((5,)),
            dma((4 * CHUNKS,)),
            dma((4 * CHUNKS,)),
            dma((2, 3)),
            dma((2, 3)),
            dma((CHUNKS, 3)),
            dma((CHUNKS, 3)),
            dma((CHUNKS, 3)),
            dma((CHUNKS, 3)),
            dma((CHUNKS,)),
            dma((CHUNKS,)),
            dma((6,)),
            dma((6,)),
            dma((4 * CHUNKS,)),
            dma((4 * CHUNKS,)),
            dma((14,)),
            dma((14,)),
            dma((8,)),
            dma((8,)),
        ],
        compiler_params=pltpu.CompilerParams(
            collective_id=0, has_side_effects=True, vmem_limit_bytes=56 * 1024 * 1024
        ),
        cost_estimate=pl.CostEstimate(flops=5_000_000_000, bytes_accessed=6_000_000, transcendentals=800_000),
        name="mesh_attention",
    )(neighbor_ids, queries, key_vectors, value_vectors, upstream, w_out)
    return tuple(out)


def solution(mesh):
    rows = P("rep", "shard", None)
    return jax.shard_map(
        per_device,
        mesh=mesh,
        in_specs=(rows, rows, rows, rows, rows, P("shard", None)),
        out_specs=(rows, rows, rows, rows, P("shard", None)),
        check_vma=False,
    )
```

```python
import functools

import jax
import jax.numpy as jnp
from jax import lax
from jax.experimental import pallas as pl
from jax.experimental.pallas import tpu as pltpu
from jax.sharding import PartitionSpec as P

HEADS = 16
DH = 128
PATCH = 128
WIDTH = 2048
HALF = 1024
CHUNKS = 4
CW = WIDTH // CHUNKS
TW = HALF // CHUNKS
ORDER = (0, 1, 3, 2)
MESH = pl.DeviceIdType.MESH
F32 = jnp.float32
BF16 = jnp.bfloat16


def remote(src, dst, send, recv, target):
    return pltpu.make_async_remote_copy(
        src_ref=src, dst_ref=dst, send_sem=send, recv_sem=recv, device_id=target, device_id_type=MESH
    )


def kernel(
    factor,
    ids_ref,
    q_hbm,
    k_hbm,
    v_hbm,
    u_hbm,
    w_hbm,
    proj_ref,
    gq_ref,
    gk_ref,
    gv_ref,
    gw_ref,
    q_s,
    kw,
    vw,
    ubuf,
    tile,
    gsend,
    grecv,
    att,
    abuf,
    psend,
    precv,
    prob,
    prob_half,
    kts,
    vts,
    ktr,
    vtr,
    gw,
    ds,
    dr,
    xs,
    xr,
    zs,
    zr,
    fs,
    fr,
    local_sem,
    kv_send,
    kv_recv,
    y_send,
    y_recv,
    a_send,
    a_recv,
    gy_send,
    gy_recv,
    wd_send,
    wd_recv,
    w_send,
    w_recv,
    t_send,
    t_recv,
    g_send,
    g_recv,
    f_send,
    f_recv,
):
    s = lax.axis_index("shard")
    r = lax.axis_index("rep")
    c = s % 2
    zl = (s // 2) % 4
    x = s // 8
    y = r % 4
    zh = r // 4
    z = zh * 4 + zl
    a = y // 2
    b = y % 2
    par = zl % 2
    zz = zl // 2

    def dev(dx, dy, zpos, core):
        return (dx * 8 + (zpos % 4) * 2 + core, (zpos // 4) * 4 + dy)

    ydev = [dev(x, (y + d) % 4, z, c) for d in range(4)]
    xdev = [dev((x + d) % 4, y, z, c) for d in range(4)]
    zdev = [dev(x, y, (z + d) % 8, c) for d in range(8)]
    sib = dev(x, y, z, 1 - c)
    left = (jnp.maximum(s - 1, 0), r)
    right = (jnp.minimum(s + 1, 31), r)
    x_left = jnp.maximum(s - 1, 0) // 8
    x_right = jnp.minimum(s + 1, 31) // 8
    has_left = s > 0
    has_right = s < 31

    loads = [
        pltpu.make_async_copy(q_hbm.at[0], q_s, local_sem.at[0]),
        pltpu.make_async_copy(k_hbm.at[0], kw.at[pl.ds(PATCH, PATCH)], local_sem.at[1]),
        pltpu.make_async_copy(v_hbm.at[0], vw.at[pl.ds(PATCH, PATCH)], local_sem.at[2]),
        pltpu.make_async_copy(
            u_hbm.at[0, :, pl.ds(pl.multiple_of(b * HALF, HALF), HALF)], ubuf.at[y], local_sem.at[3]
        ),
    ]
    for copy in loads:
        copy.start()
    wcols = pl.ds(pl.multiple_of(b * HALF, HALF), HALF)
    own_w = pltpu.make_async_copy(w_hbm.at[:, wcols], tile.at[2 * x + zz, c], local_sem.at[4])

    @pl.when(par == a)
    def _():
        own_w.start()

    barrier = pltpu.get_barrier_semaphore()

    def greet(target):
        pl.semaphore_signal(barrier, inc=1, device_id=target, device_id_type=MESH)

    for d in range(1, 4):
        greet(ydev[d])
        greet(xdev[d])
    for d in range(1, 8):
        greet(zdev[d])
    greet(sib)

    @pl.when(has_left)
    def _():
        greet(left)

    @pl.when(has_right)
    def _():
        greet(right)

    for bb in range(2):
        for zlow in range(2):
            for zhigh in range(2):
                sy = 2 * par + bb
                szl = 2 * zz + zlow
                same = (sy == y) & (szl == zl) & (zhigh == zh)

                @pl.when(jnp.logical_not(same))
                def _(sy=sy, szl=szl, zhigh=zhigh):
                    greet(dev(x, sy, zhigh * 4 + szl, c))

    wait_for = (
        14
        + jnp.where(has_left, 1, 0)
        + jnp.where(has_right, 1, 0)
        + jnp.where(par == a, 7, 8)
    )
    pl.semaphore_wait(barrier, wait_for)

    zoff = [1, 7, jnp.where(c == 0, 2, 6)]

    @pl.when(par == a)
    def _():
        for i, d in enumerate(zoff):
            remote(
                w_hbm.at[:, wcols],
                tile.at[2 * x + zz, c],
                w_send.at[i],
                w_recv.at[i],
                dev(x, y, (z + d) % 8, c),
            ).start()

    def chunk(at_x, i):
        return (at_x + ORDER[i]) % 4

    def halo(i, k, direction, at_x):
        src, dst = ((k_hbm, kw), (v_hbm, vw))[k]
        cols = pl.ds(pl.multiple_of(chunk(at_x, i) * CW, CW), CW)
        rows = pl.ds(0 if direction else 2 * PATCH, PATCH)
        index = (i * 2 + k) * 2 + direction
        return remote(
            src.at[0, :, cols],
            dst.at[rows, cols],
            kv_send.at[index],
            kv_recv.at[index],
            right if direction else left,
        )

    def halo_start(i):
        for k in range(2):

            @pl.when(has_left)
            def _(k=k):
                halo(i, k, 0, x_left).start()

            @pl.when(has_right)
            def _(k=k):
                halo(i, k, 1, x_right).start()

    def halo_wait(i):
        for k in range(2):

            @pl.when(has_left)
            def _(k=k):
                halo(i, k, 1, x).wait_recv()

            @pl.when(has_right)
            def _(k=k):
                halo(i, k, 0, x).wait_recv()

    for i in range(CHUNKS):
        halo_start(i)

    def ycopy(kind, d, src, dst_buf, slot):
        return remote(src, dst_buf.at[slot], y_send.at[kind, d - 1], y_recv.at[kind, d - 1], ydev[d])

    def u_piece(d):
        bb = ((y + d) % 4) % 2
        return u_hbm.at[0, :, pl.ds(pl.multiple_of(bb * HALF, HALF), HALF)]

    for d in (1, 3, 2):
        ycopy(0, d, u_piece(d), ubuf, y).start()

    def ywait_recv(kind, d, src, dst_buf):
        ycopy(kind, d, src, dst_buf, (y - d + 4) % 4).wait_recv()

    @pl.when(jnp.logical_not(has_left))
    def _():
        kw[0:PATCH, :] = jnp.zeros((PATCH, WIDTH), BF16)
        vw[0:PATCH, :] = jnp.zeros((PATCH, WIDTH), BF16)
        ktr[0] = jnp.zeros((PATCH, WIDTH), BF16)
        vtr[0] = jnp.zeros((PATCH, WIDTH), BF16)

    @pl.when(jnp.logical_not(has_right))
    def _():
        kw[2 * PATCH :, :] = jnp.zeros((PATCH, WIDTH), BF16)
        vw[2 * PATCH :, :] = jnp.zeros((PATCH, WIDTH), BF16)
        ktr[1] = jnp.zeros((PATCH, WIDTH), BF16)
        vtr[1] = jnp.zeros((PATCH, WIDTH), BF16)

    def wz_wait(i):
        d = zoff[i]
        szl = (z - d + 8) % 4
        remote(
            w_hbm.at[:, wcols],
            tile.at[2 * x + szl // 2, c],
            w_send.at[i],
            w_recv.at[i],
            sib,
        ).wait_recv()

    @pl.when(par == a)
    def _():
        own_w.wait()
        wz_wait(2)

    @pl.when(par != a)
    def _():
        wz_wait(0)
        wz_wait(1)

    def wx(d):
        part = tile.at[pl.ds(2 * x, 2), c]
        return remote(part, part, w_send.at[2 + d], w_recv.at[2 + d], xdev[d])

    def wx_wait(d):
        part = tile.at[pl.ds(2 * ((x - d + 4) % 4), 2), c]
        remote(part, part, w_send.at[2 + d], w_recv.at[2 + d], xdev[d]).wait_recv()

    for d in (1, 3, 2):
        wx(d).start()

    for copy in loads[:3]:
        copy.wait()
    left_ok = ids_ref[0, 0, 0] != s
    right_ok = ids_ref[0, 0, 1] != s
    at = lax.broadcasted_iota(jnp.int32, (PATCH, 3 * PATCH), 1)
    allowed = ((at >= PATCH) | left_ok) & ((at < 2 * PATCH) | right_ok)
    scaling = DH ** (-0.5)
    per = HEADS // 2 // CHUNKS

    def forward_head(h, half, t):
        cols = pl.ds(pl.multiple_of(h * DH, DH), DH)
        scores = (
            lax.dot_general(q_s[:, cols], kw[:, cols], (((1,), (1,)), ((), ())), preferred_element_type=F32)
            * scaling
        )
        highest = jnp.max(jnp.where(allowed, scores, -jnp.inf), axis=-1, keepdims=True)
        numer = jnp.where(allowed, jnp.exp(scores - highest), 0.0)
        total = jnp.sum(numer, axis=-1, keepdims=True)
        p = numer / total
        ph = p.astype(BF16)
        prob[h] = p
        prob_half[h] = ph
        out = jnp.dot(ph, vw[:, cols], preferred_element_type=F32)
        att[half, :, pl.ds(pl.multiple_of(t * DH, DH), DH)] = out.astype(BF16)

    def tcols(i):
        return pl.ds(pl.multiple_of(chunk(x, i) * TW, TW), TW)

    def a_copy(i, d, slot):
        return remote(
            att.at[((y + d) % 4) // 2, :, tcols(i)],
            abuf.at[slot, :, tcols(i)],
            a_send.at[i, d - 1],
            a_recv.at[i, d - 1],
            ydev[d],
        )

    def forward(i):
        halo_wait(i)
        first = chunk(x, i) * per

        @pl.loop(0, per)
        def _(n):
            for half in range(2):
                forward_head(2 * (first + n) + half, half, first + n)

        for d in (1, 3, 2):
            a_copy(i, d, y).start()
        abuf[y, :, tcols(i)] = att[a, :, tcols(i)]

    def wd_copy(i, core):
        part = tile.at[pl.ds(2 * chunk(x, i), 2), core]
        return remote(part, part, wd_send.at[i], wd_recv.at[i], sib)

    def tile_ready(i):
        if i > 0:
            wx_wait((4 - ORDER[i]) % 4)
        wd_copy(i, c).start()

    def g_copy(i, d, slot):
        return remote(
            gsend.at[(y + d) % 4, :, tcols(i)],
            grecv.at[slot, :, tcols(i)],
            gy_send.at[i, d - 1],
            gy_recv.at[i, d - 1],
            ydev[d],
        )

    def upstream_part(i):
        wd_copy(i, 1 - c).wait_recv()
        rows = tile[pl.ds(2 * chunk(x, i), 2)].reshape(TW, HALF)
        nodes = ubuf[...].reshape(4 * PATCH, HALF)
        part = lax.dot_general(nodes, rows, (((1,), (1,)), ((), ())), preferred_element_type=F32)
        gsend[:, :, tcols(i)] = part.astype(BF16).reshape(4, PATCH, TW)
        for d in (1, 3, 2):
            g_copy(i, d, y).start()
        grecv[y, :, tcols(i)] = gsend[y, :, tcols(i)]

    def d_copy(i):
        return remote(ds.at[i], dr.at[i], g_send.at[i], g_recv.at[i], sib)

    def x_copy(i):
        d = ORDER[i]
        return remote(xs.at[i - 1], xr.at[d - 1], g_send.at[3 + d], g_recv.at[3 + d], xdev[d])

    def gradient(i):
        for d in (1, 3, 2):
            a_copy(i, d, (y - d + 4) % 4).wait_recv()
        cols_a = abuf[:, :, tcols(i)].reshape(4 * PATCH, TW)
        nodes_u = ubuf[...].reshape(4 * PATCH, HALF)
        part = lax.dot_general(cols_a, nodes_u, (((0,), (0,)), ((), ())), preferred_element_type=F32)
        gw[i] = part.reshape(2, 2, 64, HALF)
        ds[i] = gw[i, :, 1 - c].astype(BF16)
        d_copy(i).start()

    def over_x(i):
        d_copy(i).wait_recv()
        xs[i - 1] = (gw[i, :, c] + dr[i].astype(F32)).astype(BF16)
        x_copy(i).start()

    def term(i, k, direction, at_x):
        src, dst = ((kts, ktr), (vts, vtr))[k]
        cols = pl.ds(pl.multiple_of(chunk(at_x, i) * CW, CW), CW)
        index = (i * 2 + k) * 2 + direction
        return remote(
            src.at[2 * direction, :, cols],
            dst.at[1 - direction, :, cols],
            t_send.at[index],
            t_recv.at[index],
            right if direction else left,
        )

    def backward_head(h, half, t):
        cols = pl.ds(pl.multiple_of(h * DH, DH), DH)
        tc = pl.ds(pl.multiple_of(t * DH, DH), DH)
        ga = (grecv[2 * half, :, tc].astype(F32) + grecv[2 * half + 1, :, tc].astype(F32)).astype(BF16)
        p = prob[h]
        pg = lax.dot_general(ga, vw[:, cols], (((1,), (1,)), ((), ())), preferred_element_type=F32)
        delta = jnp.sum(p * pg, axis=-1, keepdims=True)
        sg = (p * (pg - delta)).astype(BF16)
        gq_ref[0, :, cols] = (jnp.dot(sg, kw[:, cols], preferred_element_type=F32) * scaling).astype(BF16)
        kt = (
            lax.dot_general(sg, q_s[:, cols], (((0,), (0,)), ((), ())), preferred_element_type=F32) * scaling
        ).astype(BF16)
        vt = lax.dot_general(
            prob_half[h], ga, (((0,), (0,)), ((), ())), preferred_element_type=F32
        ).astype(BF16)
        kts[:, :, cols] = kt.reshape(3, PATCH, DH)
        vts[:, :, cols] = vt.reshape(3, PATCH, DH)

    def backward(i):
        first = chunk(x, i) * per
        for d in (1, 3, 2):
            g_copy(i, d, (y - d + 4) % 4).wait_recv()

        @pl.loop(0, per)
        def _(n):
            for half in range(2):
                backward_head(2 * (first + n) + half, half, first + n)

        for k in range(2):

            @pl.when(has_left)
            def _(k=k):
                term(i, k, 0, x).start()

            @pl.when(has_right)
            def _(k=k):
                term(i, k, 1, x).start()

    tile_ready(0)
    forward(0)
    loads[3].wait()
    for d in (1, 3, 2):
        ywait_recv(0, d, u_piece(d), ubuf)
    upstream_part(0)
    tile_ready(1)
    forward(1)
    upstream_part(1)
    gradient(0)
    tile_ready(2)
    forward(2)
    upstream_part(2)
    gradient(1)
    tile_ready(3)
    forward(3)
    upstream_part(3)
    over_x(1)
    gradient(2)
    backward(0)
    over_x(2)
    gradient(3)
    backward(1)
    over_x(3)

    nodes_a = abuf[...].reshape(4 * PATCH, HALF)
    weights = tile[...].reshape(HALF, HALF)
    for j in range(4):
        part = jnp.dot(nodes_a, weights[:, 256 * j : 256 * j + 256], preferred_element_type=F32)
        psend[:, :, 256 * j : 256 * j + 256] = part.astype(BF16).reshape(4, PATCH, 256)
    for d in (1, 3, 2):
        ycopy(1, d, psend.at[(y + d) % 4], precv, y).start()
    precv[y] = psend[y]

    backward(2)

    d_copy(0).wait_recv()
    own = gw[0, :, c] + dr[0].astype(F32)
    for i in range(1, CHUNKS):
        x_copy(i).wait_recv()
    for d in range(3):
        own += xr[d].astype(F32)
    zs[...] = own.astype(BF16)

    def z_piece(d):
        to = (z + d) % 8
        quarter = (to // 4) * 2 + to % 2
        return zs.at[(to % 4) // 2, pl.ds(pl.multiple_of(quarter * 16, 16), 16)]

    def z_copy(d):
        return remote(z_piece(d), zr.at[d - 1], g_send.at[6 + d], g_recv.at[6 + d], zdev[d])

    for d in (4, 3, 5, 2, 6, 1, 7):
        z_copy(d).start()

    backward(3)

    quarter = zh * 2 + par
    mine = zs[zz, pl.ds(pl.multiple_of(quarter * 16, 16), 16)].astype(F32)
    for d in range(1, 8):
        z_copy(d).wait_recv()
    for d in range(7):
        mine += zr[d].astype(F32)
    fs[...] = (mine * factor).astype(BF16)

    szl = 2 * zz + a

    def spread(zhigh, dy, slot):
        return remote(
            fs,
            fr.at[quarter, b],
            f_send.at[slot],
            f_recv.at[2 * quarter + b],
            dev(x, dy, zhigh * 4 + szl, c),
        )

    def spread_same(zhigh, dy):
        return (par == a) & (zhigh == zh) & (dy == y)

    for zhigh in range(2):
        for dy in range(4):

            @pl.when(jnp.logical_not(spread_same(zhigh, dy)))
            def _(zhigh=zhigh, dy=dy):
                spread(zhigh, dy, zhigh * 4 + dy).start()

    @pl.when(par == a)
    def _():
        fr[quarter, b] = fs[...]

    for d in (1, 3, 2):
        ywait_recv(1, d, psend.at[(y + d) % 4], precv)
    for bb in range(2):
        proj_ref[0, :, bb * HALF : (bb + 1) * HALF] = (
            precv[bb].astype(F32) + precv[2 + bb].astype(F32)
        ).astype(BF16)

    for i in range(CHUNKS):
        for k in range(2):

            @pl.when(has_left)
            def _(i=i, k=k):
                term(i, k, 1, x_left).wait_recv()

            @pl.when(has_right)
            def _(i=i, k=k):
                term(i, k, 0, x_right).wait_recv()

    gk_ref[0] = (kts[1].astype(F32) + ktr[0].astype(F32) + ktr[1].astype(F32)).astype(BF16)
    gv_ref[0] = (vts[1].astype(F32) + vtr[0].astype(F32) + vtr[1].astype(F32)).astype(BF16)

    for qq in range(4):
        for bb in range(2):
            same = (par == a) & (qq == quarter) & (bb == b)

            @pl.when(jnp.logical_not(same))
            def _(qq=qq, bb=bb):
                remote(
                    fs, fr.at[qq, bb], f_send.at[0], f_recv.at[2 * qq + bb], sib
                ).wait_recv()

    for qq in range(4):
        for bb in range(2):
            gw_ref[16 * qq : 16 * qq + 16, bb * HALF : (bb + 1) * HALF] = fr[qq, bb].astype(F32)

    @pl.when(par == a)
    def _():
        for i in range(3):
            remote(w_hbm.at[:, wcols], tile.at[2 * x + zz, c], w_send.at[i], w_recv.at[i], sib).wait_send()

    for d in range(1, 4):
        wx(d).wait_send()
        ycopy(0, d, u_piece(d), ubuf, y).wait_send()
        for i in range(CHUNKS):
            a_copy(i, d, y).wait_send()
            g_copy(i, d, y).wait_send()
        ycopy(1, d, psend.at[(y + d) % 4], precv, y).wait_send()
        x_copy(d).wait_send()
    for i in range(CHUNKS):
        d_copy(i).wait_send()
        wd_copy(i, c).wait_send()
    for d in range(1, 8):
        z_copy(d).wait_send()
    for i in range(CHUNKS):
        for k in range(2):

            @pl.when(has_left)
            def _(i=i, k=k):
                halo(i, k, 0, x_left).wait_send()
                term(i, k, 0, x).wait_send()

            @pl.when(has_right)
            def _(i=i, k=k):
                halo(i, k, 1, x_right).wait_send()
                term(i, k, 1, x).wait_send()

    for zhigh in range(2):
        for dy in range(4):

            @pl.when(jnp.logical_not(spread_same(zhigh, dy)))
            def _(zhigh=zhigh, dy=dy):
                spread(zhigh, dy, zhigh * 4 + dy).wait_send()


def place(*refs):
    sources, targets, staged, sems = refs[:5], refs[5:10], refs[10:15], refs[15]
    reads = [pltpu.make_async_copy(sources[i], staged[i], sems.at[0, i]) for i in range(5)]
    writes = [pltpu.make_async_copy(staged[i], targets[i], sems.at[1, i]) for i in range(5)]
    for copy in reads:
        copy.start()
    for read, write in zip(reads, writes):
        read.wait()
        write.start()
    for copy in writes:
        copy.wait()


def per_device(queries, key_vectors, value_vectors, neighbor_ids, upstream, w_out):
    factor = float(8 * 4096) ** (-0.5)
    rows = jax.ShapeDtypeStruct((1, PATCH, WIDTH), BF16)
    dma = pltpu.SemaphoreType.DMA
    vmem = pltpu.VMEM
    out = pl.pallas_call(
        functools.partial(kernel, factor),
        out_shape=(rows, rows, rows, rows, jax.ShapeDtypeStruct((64, WIDTH), F32)),
        in_specs=[pl.BlockSpec(memory_space=pltpu.SMEM)] + [pl.BlockSpec(memory_space=pl.ANY)] * 5,
        out_specs=[pl.BlockSpec(memory_space=pltpu.VMEM)] * 5,
        scratch_shapes=[
            vmem((PATCH, WIDTH), BF16),
            vmem((3 * PATCH, WIDTH), BF16),
            vmem((3 * PATCH, WIDTH), BF16),
            vmem((4, PATCH, HALF), BF16),
            vmem((8, 2, 64, HALF), BF16),
            vmem((4, PATCH, HALF), BF16),
            vmem((4, PATCH, HALF), BF16),
            vmem((2, PATCH, HALF), BF16),
            vmem((4, PATCH, HALF), BF16),
            vmem((4, PATCH, HALF), BF16),
            vmem((4, PATCH, HALF), BF16),
            vmem((HEADS, PATCH, 3 * PATCH), F32),
            vmem((HEADS, PATCH, 3 * PATCH), BF16),
            vmem((3, PATCH, WIDTH), BF16),
            vmem((3, PATCH, WIDTH), BF16),
            vmem((2, PATCH, WIDTH), BF16),
            vmem((2, PATCH, WIDTH), BF16),
            vmem((CHUNKS, 2, 2, 64, HALF), F32),
            vmem((CHUNKS, 2, 64, HALF), BF16),
            vmem((CHUNKS, 2, 64, HALF), BF16),
            vmem((3, 2, 64, HALF), BF16),
            vmem((3, 2, 64, HALF), BF16),
            vmem((2, 64, HALF), BF16),
            vmem((7, 16, HALF), BF16),
            vmem((16, HALF), BF16),
            vmem((4, 2, 16, HALF), BF16),
            dma((5,)),
            dma((4 * CHUNKS,)),
            dma((4 * CHUNKS,)),
            dma((2, 3)),
            dma((2, 3)),
            dma((CHUNKS, 3)),
            dma((CHUNKS, 3)),
            dma((CHUNKS, 3)),
            dma((CHUNKS, 3)),
            dma((CHUNKS,)),
            dma((CHUNKS,)),
            dma((6,)),
            dma((6,)),
            dma((4 * CHUNKS,)),
            dma((4 * CHUNKS,)),
            dma((14,)),
            dma((14,)),
            dma((8,)),
            dma((8,)),
        ],
        compiler_params=pltpu.CompilerParams(
            collective_id=0, has_side_effects=True, vmem_limit_bytes=56 * 1024 * 1024
        ),
        cost_estimate=pl.CostEstimate(flops=5_000_000_000, bytes_accessed=6_000_000, transcendentals=800_000),
        name="mesh_attention",
    )(neighbor_ids, queries, key_vectors, value_vectors, upstream, w_out)
    anywhere = pl.BlockSpec(memory_space=pl.ANY)
    return pl.pallas_call(
        place,
        out_shape=[jax.ShapeDtypeStruct(o.shape, o.dtype) for o in out],
        in_specs=[anywhere] * 5,
        out_specs=[anywhere] * 5,
        scratch_shapes=[vmem(o.shape, o.dtype) for o in out] + [dma((2, 5))],
        name="place",
    )(*out)


def solution(mesh):
    rows = P("rep", "shard", None)
    return jax.shard_map(
        per_device,
        mesh=mesh,
        in_specs=(rows, rows, rows, rows, rows, P("shard", None)),
        out_specs=(rows, rows, rows, rows, P("shard", None)),
        check_vma=False,
    )
```
